128 devices in a mesh: batch: 8 (over y_hi, z), feat: 16 (over x, y_lo, core).
Axes of the slice: x: 4, y: 4 (y_hi: 2, y_lo: 2; y = y_hi * 2 + y_lo), z: 4, core: 2. Of those that a mesh axis runs over, the one named last changes fastest.
Arguments:
- view_a: bfloat16 [4096, 8192], P('batch', 'feat'), may hold values from -100 to 100
- view_b: bfloat16 [4096, 8192], P('batch', 'feat'), may hold values from -100 to 100
Outputs:
- grad_a: bfloat16 [4096, 8192], P('batch', 'feat')
- grad_b: bfloat16 [4096, 8192], P('batch', 'feat')
- loss: float32 [], replicated
The draws below stay inside these ranges and needn't reach their ends.
All inputs are finite; a program needn't handle non-finite values.
Results may differ from the reference program's by a relative error of at most 0.0069.
Values may be sent and summed in bfloat16 or wider, within the bound.
No kernel may reach another device: no remote copies, remote signals or barrier semaphores. Data moves between devices by JAX's collectives and lax.ppermute only.
A program may use at most 128 MiB of HBM per device.

```python
import math
import jax
import jax.numpy as jnp
from jax import lax

D = 8192
SAMPLES = 4096


def common(key):
    keys = jax.random.split(key, 4)
    index = jnp.arange(SAMPLES, dtype=jnp.float32)[:, None]
    row_scale = jnp.exp(math.log(3.0) * index / (SAMPLES - 1)) * jax.random.uniform(keys[0], (SAMPLES, 1), jnp.float32, 0.8, 1.25)
    col_scale = jnp.exp(jax.random.uniform(keys[1], (1, D), jnp.float32, math.log(0.3), math.log(3.0)))
    offset = jax.random.uniform(keys[2], (1, D), jnp.float32, -1.0, 1.0)
    gauss = jnp.clip(jax.random.normal(keys[3], (SAMPLES, D), jnp.float32), -6.0, 6.0)
    base = gauss
    return (offset, row_scale * col_scale, base)


def make_view(key, salt):
    offset, scaling, base = common(key)
    own_key = jax.random.fold_in(key, salt)
    noise = jnp.clip(jax.random.normal(own_key, base.shape, jnp.float32), -6.0, 6.0)
    return (offset + scaling * (base + 0.15 * noise)).astype(jnp.bfloat16)


def draw_view_a(key, part):
    return make_view(key, 11)


def draw_view_b(key, part):
    return make_view(key, 23)


def setup_inputs(seed: int = 0) -> dict:
    key_of = jax.random.split(jax.random.key(seed), 3)
    return {
        "view_a": draw_view_a(jax.random.fold_in(key_of[2], 71), 0),
        "view_b": draw_view_b(jax.random.fold_in(key_of[2], 71), 0),
    }


def view_parts(zview):
    zf = zview.astype(jnp.float32)
    mean = lax.optimization_barrier(jnp.sum(zf, axis=0)) / SAMPLES
    cent = zf - mean
    var = lax.optimization_barrier(jnp.sum(cent * cent, axis=0)) / (SAMPLES - 1)
    std = jnp.sqrt(var + 0.0001)
    cent_low = cent.astype(jnp.bfloat16)
    gram = jnp.dot(cent_low, cent_low.T, preferred_element_type=jnp.float32)
    frob = jnp.sum(gram * gram)
    gram_low = gram.astype(jnp.bfloat16)
    inner = jnp.dot(gram_low, cent_low, preferred_element_type=jnp.float32) / (SAMPLES - 1)
    ratio = SAMPLES / (SAMPLES - 1)
    term = ratio * (inner - cent * var) - 3.125 * ratio * jnp.where(std < 1.0, 1.0 / std, 0.0) * cent
    column_part = 12.5 * jnp.sum(jax.nn.relu(1.0 - std)) - jnp.sum(var * var)
    return (zf, term, column_part, frob)

def reference(view_a, view_b):
    first, term_a, col_a, frob_a = view_parts(view_a)
    second, term_b, col_b, frob_b = view_parts(view_b)
    diff = first - second
    grad_a = (term_a + 12.5 * diff).astype(jnp.bfloat16)
    grad_b = (term_b - 12.5 * diff).astype(jnp.bfloat16)
    loss = 25.0 * jnp.sum(diff * diff) / (SAMPLES * D) + (col_a + col_b) / D + (frob_a + frob_b) / ((SAMPLES - 1.0) ** 2 * D)
    return (grad_a, grad_b, loss)
```

```python
import jax
import jax.numpy as jnp
from jax import lax
from jax.sharding import Mesh, PartitionSpec as P

D = 8192
F32 = jnp.float32
BF16 = jnp.bfloat16
AXES = ("yh", "z", "x", "yl", "c")
SIZES = (2, 4, 4, 2, 2)
COUNT = dict(zip(AXES, SIZES, strict=True))


def shift(value, axis, step):
    size = COUNT[axis]
    return lax.ppermute(value, axis, [(i, (i + step) % size) for i in range(size)])


def gather_small(value, axes, size):
    return lax.all_to_all(jnp.broadcast_to(value, (size,) + value.shape), axes, 0, 0)


def nt(lhs, rhs):
    return lax.dot_general(lhs, rhs, (((1,), (1,)), ((), ())), preferred_element_type=F32)


def reduce_gram(part):
    n = part.shape[1]
    pieces = part.astype(BF16).reshape(4, 2, 64, n)
    got = lax.all_to_all(pieces, "x", 0, 0)
    total = jnp.sum(got.astype(F32), axis=0)
    yl = lax.axis_index("yl")
    keep = jnp.where(yl == 0, total[0], total[1])
    send = jnp.where(yl == 0, total[1], total[0]).astype(BF16)
    return keep + shift(send, "yl", 1).astype(F32)


def gather_gram(low):
    n = low.shape[1]
    other = shift(low, "yl", 1)
    first = lax.axis_index("yl") == 0
    pair = jnp.stack([jnp.where(first, low, other), jnp.where(first, other, low)])
    return gather_small(pair, "x", 4).reshape(512, n)


def body(view_a, view_b):
    rows = view_a.shape[0]
    samples = 4096
    divisor = float(samples - 1)
    core0 = lax.axis_index("c") == 0

    got_a = shift(view_a, "c", 1)
    got_b = shift(view_b, "c", 1)
    mine = jnp.concatenate(
        [jnp.where(core0, view_a, view_b), jnp.where(core0, got_a, got_b)], axis=1
    )
    other = jnp.concatenate(
        [jnp.where(core0, view_b, view_a), jnp.where(core0, got_b, got_a)], axis=1
    )

    mine32 = mine.astype(F32)
    local_sum = jnp.sum(mine32, axis=0)
    local_dev = mine32 - local_sum / rows
    local_square = jnp.sum(local_dev * local_dev, axis=0)
    stats = gather_small(jnp.stack([local_sum, local_square]), ("yh", "z"), 8)
    mean = jnp.sum(stats[:, 0], axis=0) / samples
    apart = stats[:, 0] / rows - mean
    square = jnp.sum(stats[:, 1], axis=0) + rows * jnp.sum(apart * apart, axis=0)
    var = square / divisor
    std = jnp.sqrt(var + 0.0001)

    left = shift(mine, "z", 1)
    right = shift(mine, "z", 3)
    partner = shift(mine, "yh", 1)
    far0 = shift(left[:256], "z", 1)
    far1 = shift(right[256:], "z", 3)

    def centre(value):
        return (value.astype(F32) - mean).astype(BF16)

    cent = mine32 - mean
    own = cent.astype(BF16)
    pair = centre(partner)
    half = jnp.concatenate([own, centre(left), centre(right), centre(far0), centre(far1)])

    red_pair = reduce_gram(nt(pair, half))
    red_own = reduce_gram(nt(own, half))
    frobenius = jnp.sum(red_pair * red_pair) + jnp.sum(red_own * red_own)

    gram_pair = gather_gram(red_pair.astype(BF16))
    inner_pair = jnp.dot(gram_pair, half, preferred_element_type=F32)
    from_pair = shift(inner_pair.astype(BF16), "yh", 1)
    gram_own = gather_gram(red_own.astype(BF16))
    inner = jnp.dot(gram_own, half, preferred_element_type=F32)
    inner = (inner + from_pair.astype(F32)) / divisor

    ratio = samples / divisor
    term = (
        ratio * (inner - cent * var)
        - 3.125 * ratio * jnp.where(std < 1.0, 1.0 / std, 0.0) * cent
    )
    grad = (term + 12.5 * (mine32 - other.astype(F32))).astype(BF16)
    cols = view_a.shape[1]
    back = shift(grad[:, cols:], "c", 1)
    grad_a = jnp.where(core0, grad[:, :cols], back)
    grad_b = jnp.where(core0, back, grad[:, :cols])

    diff = view_a.astype(F32) - view_b.astype(F32)
    column_part = 12.5 * jnp.sum(jax.nn.relu(1.0 - std)) - jnp.sum(var * var)
    local_loss = (
        25.0 * jnp.sum(diff * diff) / (samples * D)
        + column_part / (D * 8)
        + frobenius / (divisor * divisor * D)
    )
    tile = jnp.full((8, 128), local_loss, F32)
    tile = jnp.sum(gather_small(tile, ("x", "yl", "c"), 16), axis=0)
    tile = jnp.sum(gather_small(tile, ("yh", "z"), 8), axis=0)
    return grad_a, grad_b, tile[0, 0]


def solution(mesh):
    fine = Mesh(mesh.devices.reshape(SIZES), AXES)
    spec = P(("yh", "z"), ("x", "yl", "c"))
    return jax.shard_map(
        body, mesh=fine, in_specs=(spec, spec), out_specs=(spec, spec, P()), check_vma=False
    )
```

```python
import jax
import jax.numpy as jnp
from jax import lax
from jax.sharding import Mesh, PartitionSpec as P

D = 8192
F32 = jnp.float32
BF16 = jnp.bfloat16
AXES = ("yh", "z", "x", "yl", "c")
SIZES = (2, 4, 4, 2, 2)
COUNT = dict(zip(AXES, SIZES, strict=True))


def shift(value, axis, step):
    size = COUNT[axis]
    return lax.ppermute(value, axis, [(i, (i + step) % size) for i in range(size)])


def gather_small(value, axes, size):
    return lax.all_to_all(jnp.broadcast_to(value, (size,) + value.shape), axes, 0, 0)


def swap(value, axis, mask):
    return lax.ppermute(value, axis, [(i, i ^ mask) for i in range(COUNT[axis])])


def batch_shift(value, half, step):
    pairs = [(4 * y + z, 4 * (y ^ half) + (z + step) % 4) for y in range(2) for z in range(4)]
    return lax.ppermute(value, ("yh", "z"), pairs)


def nt(lhs, rhs):
    return lax.dot_general(lhs, rhs, (((1,), (1,)), ((), ())), preferred_element_type=F32)


def send_gram(part):
    pieces = part.reshape(8, part.shape[0] // 8, part.shape[1])
    return lax.all_to_all(pieces, ("x", "yl"), 0, 0)


def sum_gram(got):
    return jnp.sum(got.astype(F32), axis=0)


def spread_gram(low):
    other = shift(low, "yl", 1)
    first = lax.axis_index("yl") == 0
    return jnp.stack([jnp.where(first, low, other), jnp.where(first, other, low)])


def gather_gram(both):
    n = both.shape[2]
    prev = shift(both, "x", 1)
    succ = shift(both, "x", 3)
    far0 = shift(prev[0], "x", 1)
    far1 = shift(succ[1], "x", 3)
    x = lax.axis_index("x")
    rows = jnp.zeros((4, 2, 64, n), BF16)
    for step, block in ((0, both), (3, prev), (1, succ), (2, jnp.stack([far0, far1]))):
        rows = lax.dynamic_update_slice_in_dim(rows, block[None], (x + step) % 4, 0)
    return rows.reshape(512, n), prev


def merge(stats, axis, mask, held):
    apart = swap(stats, axis, mask)
    gap = (stats[0] - apart[0]) / held
    return jnp.stack([stats[0] + apart[0], stats[1] + apart[1] + gap * gap * (held / 2)])


def body(view_a, view_b):
    rows = view_a.shape[0]
    samples = 4096
    divisor = float(samples - 1)
    core0 = lax.axis_index("c") == 0

    got_a = shift(view_a, "c", 1)
    got_b = shift(view_b, "c", 1)
    mine = jnp.concatenate(
        [jnp.where(core0, view_a, view_b), jnp.where(core0, got_a, got_b)], axis=1
    )
    other = jnp.concatenate(
        [jnp.where(core0, view_b, view_a), jnp.where(core0, got_b, got_a)], axis=1
    )

    mine32 = mine.astype(F32)
    local_sum = jnp.sum(mine32, axis=0)
    local_dev = mine32 - local_sum / rows
    local_square = jnp.sum(local_dev * local_dev, axis=0)
    stats = jnp.stack([local_sum, local_square])
    stats = merge(merge(stats, "z", 1, 512.0), "z", 3, 1024.0)
    ring, stats = lax.optimization_barrier((mine, stats))
    stats = merge(stats, "yh", 1, 2048.0)
    sent, stats = lax.optimization_barrier((mine, stats))
    mean = stats[0] / samples
    var = stats[1] / divisor
    std = jnp.sqrt(var + 0.0001)

    left = shift(ring, "z", 1)
    right = shift(ring, "z", 3)
    partner = shift(sent, "yh", 1)
    far0 = shift(left[:256], "z", 1)
    far1 = shift(right[256:], "z", 3)

    def centre(value, mean):
        return (value.astype(F32) - mean).astype(BF16)

    cent = mine32 - mean
    own = cent.astype(BF16)
    pair = centre(partner, mean)
    near = jnp.concatenate([own, centre(right, mean)])
    far0, far1, mean1 = lax.optimization_barrier((far0, far1, mean))
    far = jnp.concatenate([centre(far0, mean1), centre(far1, mean1)])

    got_near = send_gram(nt(pair, near).astype(BF16))
    rows = jnp.stack([pair.reshape(8, 64, 1024), own.reshape(8, 64, 1024)], axis=1)
    part_far = nt(rows.reshape(1024, 1024), far).astype(BF16)
    part_own, got_near, mean2, left = lax.optimization_barrier(
        (nt(own, near).astype(BF16), got_near, mean1, left)
    )
    got_own = send_gram(part_own)
    part_far, got_own = lax.optimization_barrier((part_far, got_own))
    got_far = send_gram(part_far)
    before = centre(left, mean2)

    red_near = sum_gram(got_near)
    low_near = red_near.astype(BF16)
    turned_near = batch_shift(low_near[:, 512:], 1, 1)
    got_far, turned_near = lax.optimization_barrier((got_far, turned_near))
    red_far = sum_gram(got_far)
    low_far = red_far.astype(BF16)
    low_pair = jnp.concatenate([low_near, low_far[:64], turned_near], axis=1)
    both_pair = spread_gram(low_pair)
    red_own = sum_gram(got_own)
    low_own = red_own.astype(BF16)
    turned_own = batch_shift(low_own[:, 512:], 0, 1)
    low_own = jnp.concatenate([low_own, low_far[64:], turned_own], axis=1)

    def lanes(value):
        return jnp.sum(value.reshape(-1, 128), axis=0)

    def rows_of(value):
        return lanes(jnp.sum(value, axis=0))

    frobenius = rows_of(red_far * red_far) + sum(
        rows_of(red[:, :512] * red[:, :512]) + 2.0 * rows_of(red[:, 512:] * red[:, 512:])
        for red in (red_near, red_own)
    )
    diff = view_a.astype(F32) - view_b.astype(F32)
    column_part = lanes(12.5 * jax.nn.relu(1.0 - std) - var * var)
    loss = (
        rows_of(diff * diff) * (25.0 / (samples * D))
        + column_part * (1.0 / (D * 8))
        + frobenius * (1.0 / (divisor * divisor * D))
    )
    high = lax.reduce_precision(loss, 8, 7)
    middle = lax.reduce_precision(loss - high, 8, 7)
    low = loss - high - middle
    line = lax.broadcasted_iota(jnp.int32, (64, 128), 0)
    loss = jnp.where(line == 0, high, jnp.where(line == 1, middle, jnp.where(line == 2, low, 0.0)))
    low_own = jnp.concatenate([low_own, loss.astype(BF16)], axis=1)

    def times(gram):
        return (
            jnp.dot(gram[:, :1024], near, preferred_element_type=F32)
            + jnp.dot(gram[:, 1024:1536], far, preferred_element_type=F32)
            + lax.dot_general(
                gram[:, 1536:2048], before, (((0,), (0,)), ((), ())), preferred_element_type=F32
            )
        )

    gram_pair, came = gather_gram(both_pair)
    inner_pair = times(gram_pair).astype(BF16)
    from_pair = shift(inner_pair, "yh", 1)
    both_own, _ = lax.optimization_barrier((spread_gram(low_own), came))
    gram_own, _ = gather_gram(both_own)
    loss = jnp.sum(gram_own.reshape(8, 64, 2176)[:, :3, 2048:].astype(F32), axis=(0, 1))
    loss = jnp.broadcast_to(loss, (8, 128))
    for axis, mask in (("z", 1), ("z", 3), ("c", 1)):
        loss = loss + swap(loss, axis, mask)
    from_pair, loss = lax.optimization_barrier((from_pair, loss))
    loss = loss + swap(loss, "yh", 1)
    inner = (times(gram_own) + from_pair.astype(F32)) / divisor

    ratio = samples / divisor
    term = (
        ratio * (inner - cent * var)
        - 3.125 * ratio * jnp.where(std < 1.0, 1.0 / std, 0.0) * cent
    )
    grad = (term + 12.5 * (mine32 - other.astype(F32))).astype(BF16)
    cols = view_a.shape[1]
    back = shift(grad[:, cols:], "c", 1)
    grad_a = jnp.where(core0, grad[:, :cols], back)
    grad_b = jnp.where(core0, back, grad[:, :cols])

    return grad_a, grad_b, jnp.sum(loss[0])


def solution(mesh):
    fine = Mesh(mesh.devices.reshape(SIZES), AXES)
    spec = P(("yh", "z"), ("x", "yl", "c"))
    return jax.shard_map(
        body, mesh=fine, in_specs=(spec, spec), out_specs=(spec, spec, P()), check_vma=False
    )
```

```python
import jax
import jax.numpy as jnp
from jax import lax
from jax.sharding import Mesh, PartitionSpec as P

D = 8192
F32 = jnp.float32
BF16 = jnp.bfloat16
AXES = ("yh", "z", "x", "yl", "c")
SIZES = (2, 4, 4, 2, 2)
COUNT = dict(zip(AXES, SIZES, strict=True))


def shift(value, axis, step):
    size = COUNT[axis]
    return lax.ppermute(value, axis, [(i, (i + step) % size) for i in range(size)])


def gather_small(value, axes, size):
    return lax.all_to_all(jnp.broadcast_to(value, (size,) + value.shape), axes, 0, 0)


def swap(value, axis, mask):
    return lax.ppermute(value, axis, [(i, i ^ mask) for i in range(COUNT[axis])])


def batch_shift(value, half, step):
    pairs = [(4 * y + z, 4 * (y ^ half) + (z + step) % 4) for y in range(2) for z in range(4)]
    return lax.ppermute(value, ("yh", "z"), pairs)


def nt(lhs, rhs):
    return lax.dot_general(lhs, rhs, (((1,), (1,)), ((), ())), preferred_element_type=F32)


def send_gram(part):
    pieces = part.reshape(8, part.shape[0] // 8, part.shape[1])
    return lax.all_to_all(pieces, ("x", "yl"), 0, 0)


def sum_gram(got):
    return jnp.sum(got.astype(F32), axis=0)


def spread_gram(low):
    other = shift(low, "yl", 1)
    first = lax.axis_index("yl") == 0
    return jnp.stack([jnp.where(first, low, other), jnp.where(first, other, low)])


def gather_gram(both):
    n = both.shape[2]
    prev = shift(both, "x", 1)
    succ = shift(both, "x", 3)
    far0 = shift(prev[0], "x", 1)
    far1 = shift(succ[1], "x", 3)
    x = lax.axis_index("x")
    rows = jnp.zeros((4, 2, 64, n), BF16)
    for step, block in ((0, both), (3, prev), (1, succ), (2, jnp.stack([far0, far1]))):
        rows = lax.dynamic_update_slice_in_dim(rows, block[None], (x + step) % 4, 0)
    return rows.reshape(512, n), prev


def merge(stats, axis, mask, held):
    apart = swap(stats, axis, mask)
    gap = (stats[0] - apart[0]) / held
    return jnp.stack([stats[0] + apart[0], stats[1] + apart[1] + gap * gap * (held / 2)])


def body(view_a, view_b):
    rows = view_a.shape[0]
    samples = 4096
    divisor = float(samples - 1)
    core0 = lax.axis_index("c") == 0

    got_a = shift(view_a, "c", 1)
    got_b = shift(view_b, "c", 1)
    mine = jnp.concatenate(
        [jnp.where(core0, view_a, view_b), jnp.where(core0, got_a, got_b)], axis=1
    )
    other = jnp.concatenate(
        [jnp.where(core0, view_b, view_a), jnp.where(core0, got_b, got_a)], axis=1
    )

    mine32 = mine.astype(F32)
    local_sum = jnp.sum(mine32, axis=0)
    local_dev = mine32 - local_sum / rows
    local_square = jnp.sum(local_dev * local_dev, axis=0)
    stats = jnp.stack([local_sum, local_square])
    everyone = [stats] + [shift(stats, "z", step) for step in (1, 3, 2)]
    total = sum(one[0] for one in everyone)
    gaps = [one[0] / 512.0 - total / 2048.0 for one in everyone]
    spread = sum(one[1] + 512.0 * gap * gap for one, gap in zip(everyone, gaps, strict=True))
    stats = jnp.stack([total, spread])
    ring, stats = lax.optimization_barrier((mine, stats))
    stats = merge(stats, "yh", 1, 2048.0)
    sent, stats = lax.optimization_barrier((mine, stats))
    mean = stats[0] / samples
    var = stats[1] / divisor
    std = jnp.sqrt(var + 0.0001)

    left = shift(ring, "z", 1)
    right = shift(ring, "z", 3)
    partner = shift(sent, "yh", 1)
    far0 = shift(left[:256], "z", 1)
    far1 = shift(right[256:], "z", 3)

    def centre(value, mean):
        return (value.astype(F32) - mean).astype(BF16)

    cent = mine32 - mean
    own = cent.astype(BF16)
    part = nt(own, own).astype(BF16).reshape(4, 128, 512)
    got_self = lax.all_to_all(part, "x", 0, 0)
    partner, right, mean0, got_self = lax.optimization_barrier((partner, right, mean, got_self))
    pair = centre(partner, mean0)
    after = centre(right, mean0)
    near = jnp.concatenate([own, after])
    far0, far1, mean1 = lax.optimization_barrier((far0, far1, mean0))
    far = jnp.concatenate([centre(far0, mean1), centre(far1, mean1)])
    rows = jnp.stack([pair.reshape(8, 64, 1024), own.reshape(8, 64, 1024)], axis=1)
    part_far = nt(rows.reshape(1024, 1024), far).astype(BF16)
    part = jnp.concatenate([nt(pair, near), nt(own, after)], axis=1).astype(BF16)
    got_near = send_gram(part)
    part_far, got_near, mean2, left = lax.optimization_barrier((part_far, got_near, mean1, left))
    got_far = send_gram(part_far)
    before = centre(left, mean2)
    got_near, got_own = got_near[:, :, :1024], got_near[:, :, 1024:]

    red_near = sum_gram(got_near)
    low_near = red_near.astype(BF16)
    turned_near = batch_shift(low_near[:, 512:], 1, 1)
    got_far, turned_near = lax.optimization_barrier((got_far, turned_near))
    red_far = sum_gram(got_far)
    low_far = red_far.astype(BF16)
    low_pair = jnp.concatenate([low_near, low_far[:64], turned_near], axis=1)
    both_pair = spread_gram(low_pair)
    red_self, red_own = sum_gram(got_self), sum_gram(got_own)
    even = lax.axis_index("yl") == 0
    rest = jnp.where(even, red_self[64:], red_self[:64]).astype(BF16)
    red_self = jnp.where(even, red_self[:64], red_self[64:]) + shift(rest, "yl", 1).astype(F32)
    low_own = red_own.astype(BF16)
    turned_own = batch_shift(low_own, 0, 1)
    low_own = jnp.concatenate(
        [red_self.astype(BF16), low_own, low_far[64:], turned_own], axis=1
    )

    def lanes(value):
        return jnp.sum(value.reshape(-1, 128), axis=0)

    def rows_of(value):
        return lanes(jnp.sum(value, axis=0))

    frobenius = (
        rows_of(red_far * red_far)
        + rows_of(red_self * red_self)
        + rows_of(red_near[:, :512] * red_near[:, :512])
        + 2.0 * rows_of(red_near[:, 512:] * red_near[:, 512:] + red_own * red_own)
    )
    diff = view_a.astype(F32) - view_b.astype(F32)
    column_part = lanes(12.5 * jax.nn.relu(1.0 - std) - var * var)
    loss = (
        rows_of(diff * diff) * (25.0 / (samples * D))
        + column_part * (1.0 / (D * 8))
        + frobenius * (1.0 / (divisor * divisor * D))
    )
    high = lax.reduce_precision(loss, 8, 7)
    middle = lax.reduce_precision(loss - high, 8, 7)
    low = loss - high - middle
    line = lax.broadcasted_iota(jnp.int32, (64, 128), 0)
    loss = jnp.where(line == 0, high, jnp.where(line == 1, middle, jnp.where(line == 2, low, 0.0)))
    first = lax.axis_index("yl") == 0
    zeros = jnp.zeros((64, 128), BF16)
    loss = loss.astype(BF16)
    loss = jnp.stack([jnp.where(first, loss, zeros), jnp.where(first, zeros, loss)])
    both_pair = jnp.concatenate([both_pair, loss], axis=2)

    three = jnp.concatenate([near, far])

    def times(gram, start, stop):
        return jnp.dot(
            gram[:, :1536], three[:, start:stop], preferred_element_type=F32
        ) + lax.dot_general(
            gram[:, 1536:2048],
            before[:, start:stop],
            (((0,), (0,)), ((), ())),
            preferred_element_type=F32,
        )

    gram_pair, came = gather_gram(both_pair)
    cols = view_a.shape[1]
    inner_pair = times(gram_pair, 0, 2 * cols).astype(BF16)
    from_pair = shift(inner_pair, "yh", 1)
    both_own, _ = lax.optimization_barrier((spread_gram(low_own), came))
    gram_own, came = gather_gram(both_own)
    loss = jnp.sum(gram_pair.reshape(8, 64, 2176)[:, :3, 2048:].astype(F32), axis=(0, 1))
    loss = jnp.broadcast_to(loss, (8, 128))
    loss, _ = lax.optimization_barrier((loss, came))
    for axis, mask in (("yl", 1), ("z", 1), ("z", 3), ("c", 1), ("yh", 1)):
        loss = loss + swap(loss, axis, mask)

    ratio = samples / divisor
    weight = 3.125 * ratio * jnp.where(std < 1.0, 1.0 / std, 0.0)

    def gradient(got, start, stop):
        inner = (times(gram_own, start, stop) + got.astype(F32)) / divisor
        own_cols = cent[:, start:stop]
        term = ratio * (inner - own_cols * var[start:stop]) - weight[start:stop] * own_cols
        diff = mine32[:, start:stop] - other[:, start:stop].astype(F32)
        return (term + 12.5 * diff).astype(BF16)

    from_pair, loss = lax.optimization_barrier((from_pair, loss))
    grad = gradient(from_pair, 0, 2 * cols)
    back = shift(grad[:, cols:], "c", 1)
    keep = grad[:, :cols]
    grad_a = jnp.where(core0, keep, back)
    grad_b = jnp.where(core0, back, keep)

    return grad_a, grad_b, jnp.sum(loss[0])


def solution(mesh):
    fine = Mesh(mesh.devices.reshape(SIZES), AXES)
    spec = P(("yh", "z"), ("x", "yl", "c"))
    return jax.shard_map(
        body, mesh=fine, in_specs=(spec, spec), out_specs=(spec, spec, P()), check_vma=False
    )
```

```python
import jax
import jax.numpy as jnp
from jax import lax
from jax.sharding import Mesh, PartitionSpec as P

D = 8192
F32 = jnp.float32
BF16 = jnp.bfloat16
AXES = ("yh", "z", "x", "yl", "c")
SIZES = (2, 4, 4, 2, 2)
COUNT = dict(zip(AXES, SIZES, strict=True))


def shift(value, axis, step):
    size = COUNT[axis]
    return lax.ppermute(value, axis, [(i, (i + step) % size) for i in range(size)])


def gather_small(value, axes, size):
    return lax.all_to_all(jnp.broadcast_to(value, (size,) + value.shape), axes, 0, 0)


def swap(value, axis, mask):
    return lax.ppermute(value, axis, [(i, i ^ mask) for i in range(COUNT[axis])])


def batch_shift(value, half, step):
    pairs = [(4 * y + z, 4 * (y ^ half) + (z + step) % 4) for y in range(2) for z in range(4)]
    return lax.ppermute(value, ("yh", "z"), pairs)


def nt(lhs, rhs):
    return lax.dot_general(lhs, rhs, (((1,), (1,)), ((), ())), preferred_element_type=F32)


def send_gram(part):
    pieces = part.reshape(8, part.shape[0] // 8, part.shape[1])
    return lax.all_to_all(pieces, ("x", "yl"), 0, 0)


def sum_gram(got):
    return jnp.sum(got.astype(F32), axis=0)


def spread_gram(low):
    other = shift(low, "yl", 1)
    first = lax.axis_index("yl") == 0
    return jnp.stack([jnp.where(first, low, other), jnp.where(first, other, low)])


def gather_gram(both):
    n = both.shape[2]
    prev = shift(both, "x", 1)
    succ = shift(both, "x", 3)
    far0 = shift(prev[0], "x", 1)
    far1 = shift(succ[1], "x", 3)
    x = lax.axis_index("x")
    rows = jnp.zeros((4, 2, 64, n), BF16)
    for step, block in ((0, both), (3, prev), (1, succ), (2, jnp.stack([far0, far1]))):
        rows = lax.dynamic_update_slice_in_dim(rows, block[None], (x + step) % 4, 0)
    return rows.reshape(512, n), prev, far0


def merge(stats, axis, mask, held):
    apart = swap(stats, axis, mask)
    gap = (stats[0] - apart[0]) / held
    return jnp.stack([stats[0] + apart[0], stats[1] + apart[1] + gap * gap * (held / 2)])


def body(view_a, view_b):
    rows = view_a.shape[0]
    samples = 4096
    divisor = float(samples - 1)
    core0 = lax.axis_index("c") == 0

    got_a = shift(view_a, "c", 1)
    got_b = shift(view_b, "c", 1)
    mine = jnp.concatenate(
        [jnp.where(core0, view_a, view_b), jnp.where(core0, got_a, got_b)], axis=1
    )
    other = jnp.concatenate(
        [jnp.where(core0, view_b, view_a), jnp.where(core0, got_b, got_a)], axis=1
    )

    mine32 = mine.astype(F32)
    local_sum = jnp.sum(mine32, axis=0)
    local_dev = mine32 - local_sum / rows
    local_square = jnp.sum(local_dev * local_dev, axis=0)
    stats = jnp.stack([local_sum, local_square])
    everyone = [stats] + [shift(stats, "z", step) for step in (1, 3, 2)]
    total = sum(one[0] for one in everyone)
    gaps = [one[0] / 512.0 - total / 2048.0 for one in everyone]
    spread = sum(one[1] + 512.0 * gap * gap for one, gap in zip(everyone, gaps, strict=True))
    stats = jnp.stack([total, spread])
    ring, stats = lax.optimization_barrier((mine, stats))
    stats = merge(stats, "yh", 1, 2048.0)
    sent, stats = lax.optimization_barrier((mine, stats))
    mean = stats[0] / samples
    var = stats[1] / divisor
    std = jnp.sqrt(var + 0.0001)

    left = shift(ring, "z", 1)
    right = shift(ring, "z", 3)
    partner = shift(sent, "yh", 1)
    far0 = shift(left[:256], "z", 1)
    far1 = shift(right[256:], "z", 3)

    def centre(value, mean):
        return (value.astype(F32) - mean).astype(BF16)

    cent = mine32 - mean
    own = cent.astype(BF16)
    part = nt(own, own).astype(BF16).reshape(4, 128, 512)
    got_self = lax.all_to_all(part, "x", 0, 0)
    partner, right, mean0, got_self = lax.optimization_barrier((partner, right, mean, got_self))
    pair = centre(partner, mean0)
    after = centre(right, mean0)
    near = jnp.concatenate([own, after])
    far0, far1, mean1 = lax.optimization_barrier((far0, far1, mean0))
    far = jnp.concatenate([centre(far0, mean1), centre(far1, mean1)])
    rows = jnp.stack([pair.reshape(8, 64, 1024), own.reshape(8, 64, 1024)], axis=1)
    part_far = nt(rows.reshape(1024, 1024), far).astype(BF16)
    part = jnp.concatenate([nt(pair, near), nt(own, after)], axis=1).astype(BF16)
    got_near = send_gram(part)
    part_far, got_near, mean2, left = lax.optimization_barrier((part_far, got_near, mean1, left))
    got_far = send_gram(part_far)
    before = centre(left, mean2)
    got_near, got_own = got_near[:, :, :1024], got_near[:, :, 1024:]

    red_near = sum_gram(got_near)
    low_near = red_near.astype(BF16)
    turned_near = batch_shift(low_near[:, 512:], 1, 1)
    got_far, turned_near = lax.optimization_barrier((got_far, turned_near))
    red_far = sum_gram(got_far)
    low_far = red_far.astype(BF16)
    low_pair = jnp.concatenate([low_near, low_far[:64], turned_near], axis=1)
    both_pair = spread_gram(low_pair)
    red_self, red_own = sum_gram(got_self), sum_gram(got_own)
    even = lax.axis_index("yl") == 0
    rest = jnp.where(even, red_self[64:], red_self[:64]).astype(BF16)
    red_self = jnp.where(even, red_self[:64], red_self[64:]) + shift(rest, "yl", 1).astype(F32)
    low_own = red_own.astype(BF16)
    turned_own = batch_shift(low_own, 0, 1)
    low_own = jnp.concatenate(
        [red_self.astype(BF16), low_own, low_far[64:], turned_own], axis=1
    )

    def lanes(value):
        return jnp.sum(value.reshape(-1, 128), axis=0)

    def rows_of(value):
        return lanes(jnp.sum(value, axis=0))

    frobenius = (
        rows_of(red_far * red_far)
        + rows_of(red_self * red_self)
        + rows_of(red_near[:, :512] * red_near[:, :512])
        + 2.0 * rows_of(red_near[:, 512:] * red_near[:, 512:] + red_own * red_own)
    )
    diff = view_a.astype(F32) - view_b.astype(F32)
    column_part = lanes(12.5 * jax.nn.relu(1.0 - std) - var * var)
    loss = (
        rows_of(diff * diff) * (25.0 / (samples * D))
        + column_part * (1.0 / (D * 8))
        + frobenius * (1.0 / (divisor * divisor * D))
    )
    high = lax.reduce_precision(loss, 8, 7)
    middle = lax.reduce_precision(loss - high, 8, 7)
    low = loss - high - middle
    line = lax.broadcasted_iota(jnp.int32, (64, 128), 0)
    loss = jnp.where(line == 0, high, jnp.where(line == 1, middle, jnp.where(line == 2, low, 0.0)))
    first = lax.axis_index("yl") == 0
    zeros = jnp.zeros((64, 128), BF16)
    loss = loss.astype(BF16)
    loss = jnp.stack([jnp.where(first, loss, zeros), jnp.where(first, zeros, loss)])
    both_pair = jnp.concatenate([both_pair, loss], axis=2)

    three = jnp.concatenate([near, far])

    def times(gram, start, stop):
        return jnp.dot(
            gram[:, :1536], three[:, start:stop], preferred_element_type=F32
        ) + lax.dot_general(
            gram[:, 1536:2048],
            before[:, start:stop],
            (((0,), (0,)), ((), ())),
            preferred_element_type=F32,
        )

    gram_pair, _, came = gather_gram(both_pair)
    cols = view_a.shape[1]
    inner_pair = times(gram_pair, 0, 2 * cols).astype(BF16)
    loss = jnp.sum(gram_pair.reshape(8, 64, 2176)[:, :3, 2048:].astype(F32), axis=(0, 1))
    loss = jnp.broadcast_to(loss, (8, 128))
    loss = loss + swap(loss, "yl", 1)
    inner_pair, loss = lax.optimization_barrier((inner_pair, loss))
    from_pair = shift(inner_pair, "yh", 1)
    both_own, _ = lax.optimization_barrier((spread_gram(low_own), came))
    gram_own, came, _ = gather_gram(both_own)
    loss, _ = lax.optimization_barrier((loss, came))
    for axis, mask in (("z", 1), ("z", 3), ("c", 1)):
        loss = loss + swap(loss, axis, mask)
    inner_own, loss = lax.optimization_barrier((times(gram_own, 0, 2 * cols), loss))
    loss = loss + swap(loss, "yh", 1)
    from_pair, loss = lax.optimization_barrier((from_pair, loss))

    ratio = samples / divisor
    weight = 3.125 * ratio * jnp.where(std < 1.0, 1.0 / std, 0.0)

    inner = (inner_own + from_pair.astype(F32)) / divisor
    term = ratio * (inner - cent * var) - weight * cent
    grad = (term + 12.5 * (mine32 - other.astype(F32))).astype(BF16)
    back = shift(grad[:, cols:], "c", 1)
    keep = grad[:, :cols]
    grad_a = jnp.where(core0, keep, back)
    grad_b = jnp.where(core0, back, keep)

    return grad_a, grad_b, jnp.sum(loss[0])


def solution(mesh):
    fine = Mesh(mesh.devices.reshape(SIZES), AXES)
    spec = P(("yh", "z"), ("x", "yl", "c"))
    return jax.shard_map(
        body, mesh=fine, in_specs=(spec, spec), out_specs=(spec, spec, P()), check_vma=False
    )
```

```python
import jax
import jax.numpy as jnp
from jax import lax
from jax.sharding import Mesh, PartitionSpec as P

D = 8192
F32 = jnp.float32
BF16 = jnp.bfloat16
AXES = ("yh", "z", "x", "yl", "c")
SIZES = (2, 4, 4, 2, 2)
COUNT = dict(zip(AXES, SIZES, strict=True))


def shift(value, axis, step):
    size = COUNT[axis]
    return lax.ppermute(value, axis, [(i, (i + step) % size) for i in range(size)])


def gather_small(value, axes, size):
    return lax.all_to_all(jnp.broadcast_to(value, (size,) + value.shape), axes, 0, 0)


def swap(value, axis, mask):
    return lax.ppermute(value, axis, [(i, i ^ mask) for i in range(COUNT[axis])])


def batch_shift(value, half, step):
    pairs = [(4 * y + z, 4 * (y ^ half) + (z + step) % 4) for y in range(2) for z in range(4)]
    return lax.ppermute(value, ("yh", "z"), pairs)


def nt(lhs, rhs):
    return lax.dot_general(lhs, rhs, (((1,), (1,)), ((), ())), preferred_element_type=F32)


def send_gram(part):
    pieces = part.reshape(8, part.shape[0] // 8, part.shape[1])
    return lax.all_to_all(pieces, ("x", "yl"), 0, 0)


def sum_gram(got):
    return jnp.sum(got.astype(F32), axis=0)


def spread_gram(low):
    other = shift(low, "yl", 1)
    first = lax.axis_index("yl") == 0
    return jnp.stack([jnp.where(first, low, other), jnp.where(first, other, low)])


def gather_gram(both):
    n = both.shape[2]
    prev = shift(both, "x", 1)
    succ = shift(both, "x", 3)
    far0 = shift(prev[0], "x", 1)
    far1 = shift(succ[1], "x", 3)
    x = lax.axis_index("x")
    rows = jnp.zeros((4, 2, 64, n), BF16)
    for step, block in ((0, both), (3, prev), (1, succ), (2, jnp.stack([far0, far1]))):
        rows = lax.dynamic_update_slice_in_dim(rows, block[None], (x + step) % 4, 0)
    return rows.reshape(512, n), prev, far0


def merge(stats, axis, mask, held):
    apart = swap(stats, axis, mask)
    gap = (stats[0] - apart[0]) / held
    return jnp.stack([stats[0] + apart[0], stats[1] + apart[1] + gap * gap * (held / 2)])


def body(view_a, view_b):
    rows = view_a.shape[0]
    samples = 4096
    divisor = float(samples - 1)
    core0 = lax.axis_index("c") == 0

    got_a = shift(view_a, "c", 1)
    got_b = shift(view_b, "c", 1)
    mine = jnp.concatenate(
        [jnp.where(core0, view_a, view_b), jnp.where(core0, got_a, got_b)], axis=1
    )
    other = jnp.concatenate(
        [jnp.where(core0, view_b, view_a), jnp.where(core0, got_b, got_a)], axis=1
    )

    mine32 = mine.astype(F32)
    local_sum = jnp.sum(mine32, axis=0)
    local_dev = mine32 - local_sum / rows
    local_square = jnp.sum(local_dev * local_dev, axis=0)
    stats = jnp.stack([local_sum, local_square])
    everyone = [stats] + [shift(stats, "z", step) for step in (1, 3, 2)]
    total = sum(one[0] for one in everyone)
    gaps = [one[0] / 512.0 - total / 2048.0 for one in everyone]
    spread = sum(one[1] + 512.0 * gap * gap for one, gap in zip(everyone, gaps, strict=True))
    stats = jnp.stack([total, spread])
    ring, stats = lax.optimization_barrier((mine, stats))
    stats = merge(stats, "yh", 1, 2048.0)
    sent, stats = lax.optimization_barrier((mine, stats))
    mean = stats[0] / samples
    var = stats[1] / divisor
    std = jnp.sqrt(var + 0.0001)

    left = shift(ring, "z", 1)
    right = shift(ring, "z", 3)
    partner = shift(sent, "yh", 1)
    far0 = shift(left[:256], "z", 1)
    far1 = shift(right[256:], "z", 3)

    def centre(value, mean):
        return (value.astype(F32) - mean).astype(BF16)

    cent = mine32 - mean
    own = cent.astype(BF16)
    part = nt(own, own).astype(BF16).reshape(4, 128, 512)
    got_self = lax.all_to_all(part, "x", 0, 0)
    partner, right, mean0, got_self = lax.optimization_barrier((partner, right, mean, got_self))
    pair = centre(partner, mean0)
    after = centre(right, mean0)
    near = jnp.concatenate([own, after])
    far0, far1, mean1 = lax.optimization_barrier((far0, far1, mean0))
    far = jnp.concatenate([centre(far0, mean1), centre(far1, mean1)])
    rows = jnp.stack([pair.reshape(8, 64, 1024), own.reshape(8, 64, 1024)], axis=1)
    part_far = nt(rows.reshape(1024, 1024), far).astype(BF16)
    part = jnp.concatenate([nt(pair, near), nt(own, after)], axis=1).astype(BF16)
    got_near = send_gram(part)
    part_far, got_near, mean2, left = lax.optimization_barrier((part_far, got_near, mean1, left))
    got_far = send_gram(part_far)
    before = centre(left, mean2)
    got_near, got_own = got_near[:, :, :1024], got_near[:, :, 1024:]

    red_near = sum_gram(got_near)
    low_near = red_near.astype(BF16)
    turned_near = batch_shift(low_near[:, 512:], 1, 1)
    got_far, turned_near = lax.optimization_barrier((got_far, turned_near))
    red_far = sum_gram(got_far)
    low_far = red_far.astype(BF16)
    low_pair = jnp.concatenate([low_near, low_far[:64], turned_near], axis=1)
    both_pair = spread_gram(low_pair)
    red_self, red_own = sum_gram(got_self), sum_gram(got_own)
    even = lax.axis_index("yl") == 0
    rest = jnp.where(even, red_self[64:], red_self[:64]).astype(BF16)
    red_self = jnp.where(even, red_self[:64], red_self[64:]) + shift(rest, "yl", 1).astype(F32)
    low_own = red_own.astype(BF16)
    turned_own = batch_shift(low_own, 0, 1)
    low_own = jnp.concatenate(
        [red_self.astype(BF16), low_own, low_far[64:], turned_own], axis=1
    )

    def lanes(value):
        return jnp.sum(value.reshape(-1, 128), axis=0)

    def rows_of(value):
        return lanes(jnp.sum(value, axis=0))

    frobenius = (
        rows_of(red_far * red_far)
        + rows_of(red_self * red_self)
        + rows_of(red_near[:, :512] * red_near[:, :512])
        + 2.0 * rows_of(red_near[:, 512:] * red_near[:, 512:] + red_own * red_own)
    )
    diff = view_a.astype(F32) - view_b.astype(F32)
    column_part = lanes(12.5 * jax.nn.relu(1.0 - std) - var * var)
    loss = (
        rows_of(diff * diff) * (25.0 / (samples * D))
        + column_part * (1.0 / (D * 8))
        + frobenius * (1.0 / (divisor * divisor * D))
    )
    high = lax.reduce_precision(loss, 8, 7)
    middle = lax.reduce_precision(loss - high, 8, 7)
    low = loss - high - middle
    line = lax.broadcasted_iota(jnp.int32, (64, 128), 0)
    loss = jnp.where(line == 0, high, jnp.where(line == 1, middle, jnp.where(line == 2, low, 0.0)))
    first = lax.axis_index("yl") == 0
    zeros = jnp.zeros((64, 128), BF16)
    loss = loss.astype(BF16)
    loss = jnp.stack([jnp.where(first, loss, zeros), jnp.where(first, zeros, loss)])
    both_pair = jnp.concatenate([both_pair, loss], axis=2)

    three = jnp.concatenate([near, far])

    def times(gram, start, stop):
        return jnp.dot(
            gram[:, :1536], three[:, start:stop], preferred_element_type=F32
        ) + lax.dot_general(
            gram[:, 1536:2048],
            before[:, start:stop],
            (((0,), (0,)), ((), ())),
            preferred_element_type=F32,
        )

    gram_pair, _, came = gather_gram(both_pair)
    cols = view_a.shape[1]
    inner_pair = times(gram_pair, 0, 2 * cols).astype(BF16)
    loss = jnp.sum(gram_pair.reshape(8, 64, 2176)[:, :3, 2048:].astype(F32), axis=(0, 1))
    loss = jnp.broadcast_to(loss, (8, 128))
    loss = loss + swap(loss, "yl", 1)
    inner_pair, loss = lax.optimization_barrier((inner_pair, loss))
    from_pair = shift(inner_pair, "yh", 1)
    both_own, _ = lax.optimization_barrier((spread_gram(low_own), came))
    gram_own, came, _ = gather_gram(both_own)
    loss, _ = lax.optimization_barrier((loss, came))
    for axis, mask in (("z", 1), ("z", 3)):
        loss = loss + swap(loss, axis, mask)
    inner_own, loss = lax.optimization_barrier((times(gram_own, 0, 2 * cols), loss))
    loss = loss + swap(loss, "yh", 1)
    from_pair, loss = lax.optimization_barrier((from_pair, loss))

    ratio = samples / divisor
    weight = 3.125 * ratio * jnp.where(std < 1.0, 1.0 / std, 0.0)

    inner = (inner_own + from_pair.astype(F32)) / divisor
    term = ratio * (inner - cent * var) - weight * cent
    grad = (term + 12.5 * (mine32 - other.astype(F32))).astype(BF16)
    back = shift(grad[:, cols:], "c", 1)
    keep = grad[:, :cols]
    grad_a = jnp.where(core0, keep, back)
    grad_b = jnp.where(core0, back, keep)

    loss = loss + swap(loss, "c", 1)
    return grad_a, grad_b, jnp.sum(loss[0])


def solution(mesh):
    fine = Mesh(mesh.devices.reshape(SIZES), AXES)
    spec = P(("yh", "z"), ("x", "yl", "c"))
    return jax.shard_map(
        body, mesh=fine, in_specs=(spec, spec), out_specs=(spec, spec, P()), check_vma=False
    )
```

```python
import jax
import jax.numpy as jnp
from jax import lax
from jax.sharding import Mesh, PartitionSpec as P

D = 8192
F32 = jnp.float32
BF16 = jnp.bfloat16
AXES = ("yh", "z", "x", "yl", "c")
SIZES = (2, 4, 4, 2, 2)
COUNT = dict(zip(AXES, SIZES, strict=True))


def shift(value, axis, step):
    size = COUNT[axis]
    return lax.ppermute(value, axis, [(i, (i + step) % size) for i in range(size)])


def gather_small(value, axes, size):
    return lax.all_to_all(jnp.broadcast_to(value, (size,) + value.shape), axes, 0, 0)


def swap(value, axis, mask):
    return lax.ppermute(value, axis, [(i, i ^ mask) for i in range(COUNT[axis])])


def batch_shift(value, half, step):
    pairs = [(4 * y + z, 4 * (y ^ half) + (z + step) % 4) for y in range(2) for z in range(4)]
    return lax.ppermute(value, ("yh", "z"), pairs)


def nt(lhs, rhs):
    return lax.dot_general(lhs, rhs, (((1,), (1,)), ((), ())), preferred_element_type=F32)


def send_gram(part):
    pieces = part.reshape(8, part.shape[0] // 8, part.shape[1])
    return lax.all_to_all(pieces, ("x", "yl"), 0, 0)


def sum_gram(got):
    return jnp.sum(got.astype(F32), axis=0)


def spread_gram(low):
    other = shift(low, "yl", 1)
    first = lax.axis_index("yl") == 0
    return jnp.stack([jnp.where(first, low, other), jnp.where(first, other, low)])


def gather_gram(both):
    n = both.shape[2]
    prev = shift(both, "x", 1)
    succ = shift(both, "x", 3)
    far0 = shift(prev[0], "x", 1)
    far1 = shift(succ[1], "x", 3)
    x = lax.axis_index("x")
    rows = jnp.zeros((4, 2, 64, n), BF16)
    for step, block in ((0, both), (3, prev), (1, succ), (2, jnp.stack([far0, far1]))):
        rows = lax.dynamic_update_slice_in_dim(rows, block[None], (x + step) % 4, 0)
    return rows.reshape(512, n), prev, far0


def place(x, own, prev, opposite, succ):
    rows = jnp.zeros((4,) + own.shape, own.dtype)
    for step, block in ((0, own), (3, prev), (2, opposite), (1, succ)):
        rows = lax.dynamic_update_slice_in_dim(rows, block[None], (x + step) % 4, 0)
    return rows


def merge(stats, axis, mask, held):
    apart = swap(stats, axis, mask)
    gap = (stats[0] - apart[0]) / held
    return jnp.stack([stats[0] + apart[0], stats[1] + apart[1] + gap * gap * (held / 2)])


def body(view_a, view_b):
    rows = view_a.shape[0]
    samples = 4096
    divisor = float(samples - 1)
    core0 = lax.axis_index("c") == 0

    got_a = shift(view_a, "c", 1)
    got_b = shift(view_b, "c", 1)
    mine = jnp.concatenate(
        [jnp.where(core0, view_a, view_b), jnp.where(core0, got_a, got_b)], axis=1
    )
    other = jnp.concatenate(
        [jnp.where(core0, view_b, view_a), jnp.where(core0, got_b, got_a)], axis=1
    )

    mine32 = mine.astype(F32)
    local_sum = jnp.sum(mine32, axis=0)
    local_dev = mine32 - local_sum / rows
    local_square = jnp.sum(local_dev * local_dev, axis=0)
    stats = jnp.stack([local_sum, local_square])
    everyone = [stats] + [shift(stats, "z", step) for step in (1, 3, 2)]
    total = sum(one[0] for one in everyone)
    gaps = [one[0] / 512.0 - total / 2048.0 for one in everyone]
    spread = sum(one[1] + 512.0 * gap * gap for one, gap in zip(everyone, gaps, strict=True))
    stats = jnp.stack([total, spread])
    ring, stats = lax.optimization_barrier((mine, stats))
    stats = merge(stats, "yh", 1, 2048.0)
    sent, stats = lax.optimization_barrier((mine, stats))
    mean = stats[0] / samples
    var = stats[1] / divisor
    std = jnp.sqrt(var + 0.0001)

    left = shift(ring, "z", 1)
    right = shift(ring, "z", 3)
    partner = shift(sent, "yh", 1)
    far0 = shift(left[:256], "z", 1)
    far1 = shift(right[256:], "z", 3)

    def centre(value, mean):
        return (value.astype(F32) - mean).astype(BF16)

    cent = mine32 - mean
    own = cent.astype(BF16)
    part = nt(own, own).astype(BF16).reshape(4, 128, 512)
    got_self = lax.all_to_all(part, "x", 0, 0)
    partner, right, mean0, got_self = lax.optimization_barrier((partner, right, mean, got_self))
    pair = centre(partner, mean0)
    after = centre(right, mean0)
    near = jnp.concatenate([own, after])
    far0, far1, mean1 = lax.optimization_barrier((far0, far1, mean0))
    far = jnp.concatenate([centre(far0, mean1), centre(far1, mean1)])
    rows = jnp.stack([pair.reshape(8, 64, 1024), own.reshape(8, 64, 1024)], axis=1)
    part_far = nt(rows.reshape(1024, 1024), far).astype(BF16)
    part = jnp.concatenate([nt(pair, near), nt(own, after)], axis=1).astype(BF16)
    got_near = send_gram(part)
    part_far, got_near, mean2, left = lax.optimization_barrier((part_far, got_near, mean1, left))
    got_far = send_gram(part_far)
    before = centre(left, mean2)
    got_near, got_own = got_near[:, :, :1024], got_near[:, :, 1024:]

    red_near = sum_gram(got_near)
    low_near = red_near.astype(BF16)
    turned_near = batch_shift(low_near[:, 512:], 1, 1)
    got_far, low_near = lax.optimization_barrier((got_far, low_near))
    x = lax.axis_index("x")
    first = lax.axis_index("yl") == 0
    here = place(x, low_near, *[shift(low_near, "x", step) for step in (1, 2, 3)])
    there = shift(here, "yl", 1)
    gram_near = jnp.stack([jnp.where(first, here, there), jnp.where(first, there, here)], axis=1)
    gram_near = gram_near.reshape(512, 1024)
    red_far = sum_gram(got_far)
    low_far = red_far.astype(BF16)
    low_pair = jnp.concatenate([low_far[:64], turned_near], axis=1)
    both_pair = spread_gram(low_pair)
    red_self, red_own = sum_gram(got_self), sum_gram(got_own)
    even = lax.axis_index("yl") == 0
    rest = jnp.where(even, red_self[64:], red_self[:64]).astype(BF16)
    red_self = jnp.where(even, red_self[:64], red_self[64:]) + shift(rest, "yl", 1).astype(F32)
    low_own = red_own.astype(BF16)
    turned_own = batch_shift(low_own, 0, 1)
    low_own = jnp.concatenate(
        [red_self.astype(BF16), low_own, low_far[64:], turned_own], axis=1
    )

    def lanes(value):
        return jnp.sum(value.reshape(-1, 128), axis=0)

    def rows_of(value):
        return lanes(jnp.sum(value, axis=0))

    frobenius = (
        rows_of(red_far * red_far)
        + rows_of(red_self * red_self)
        + rows_of(red_near[:, :512] * red_near[:, :512])
        + 2.0 * rows_of(red_near[:, 512:] * red_near[:, 512:] + red_own * red_own)
    )
    diff = view_a.astype(F32) - view_b.astype(F32)
    column_part = lanes(12.5 * jax.nn.relu(1.0 - std) - var * var)
    loss = (
        rows_of(diff * diff) * (25.0 / (samples * D))
        + column_part * (1.0 / (D * 8))
        + frobenius * (1.0 / (divisor * divisor * D))
    )
    high = lax.reduce_precision(loss, 8, 7)
    middle = lax.reduce_precision(loss - high, 8, 7)
    low = loss - high - middle
    line = lax.broadcasted_iota(jnp.int32, (64, 128), 0)
    loss = jnp.where(line == 0, high, jnp.where(line == 1, middle, jnp.where(line == 2, low, 0.0)))
    first = lax.axis_index("yl") == 0
    zeros = jnp.zeros((64, 128), BF16)
    loss = loss.astype(BF16)
    loss = jnp.stack([jnp.where(first, loss, zeros), jnp.where(first, zeros, loss)])
    both_pair = jnp.concatenate([both_pair, loss], axis=2)

    three = jnp.concatenate([near, far])

    def times(gram, start, stop):
        return jnp.dot(
            gram[:, :1536], three[:, start:stop], preferred_element_type=F32
        ) + lax.dot_general(
            gram[:, 1536:2048],
            before[:, start:stop],
            (((0,), (0,)), ((), ())),
            preferred_element_type=F32,
        )

    gram_pair, _, came = gather_gram(both_pair)
    cols = view_a.shape[1]
    inner_near = jnp.dot(gram_near, near, preferred_element_type=F32)
    inner_near, gram_pair = lax.optimization_barrier((inner_near, gram_pair))
    inner_pair = (
        inner_near
        + jnp.dot(gram_pair[:, :512], far, preferred_element_type=F32)
        + lax.dot_general(
            gram_pair[:, 512:1024], before, (((0,), (0,)), ((), ())), preferred_element_type=F32
        )
    ).astype(BF16)
    loss = jnp.sum(gram_pair.reshape(8, 64, 1152)[:, :3, 1024:].astype(F32), axis=(0, 1))
    loss = jnp.broadcast_to(loss, (8, 128))
    loss = loss + swap(loss, "yl", 1)
    inner_pair, loss = lax.optimization_barrier((inner_pair, loss))
    from_pair = shift(inner_pair, "yh", 1)
    both_own, _ = lax.optimization_barrier((spread_gram(low_own), came))
    gram_own, came, _ = gather_gram(both_own)
    loss, _ = lax.optimization_barrier((loss, came))
    for axis, mask in (("z", 1), ("z", 3)):
        loss = loss + swap(loss, axis, mask)
    inner_own, loss = lax.optimization_barrier((times(gram_own, 0, 2 * cols), loss))
    loss = loss + swap(loss, "yh", 1)
    from_pair, loss = lax.optimization_barrier((from_pair, loss))

    ratio = samples / divisor
    weight = 3.125 * ratio * jnp.where(std < 1.0, 1.0 / std, 0.0)

    inner = (inner_own + from_pair.astype(F32)) / divisor
    term = ratio * (inner - cent * var) - weight * cent
    grad = (term + 12.5 * (mine32 - other.astype(F32))).astype(BF16)
    back = shift(grad[:, cols:], "c", 1)
    keep = grad[:, :cols]
    grad_a = jnp.where(core0, keep, back)
    grad_b = jnp.where(core0, back, keep)

    loss = loss + swap(loss, "c", 1)
    return grad_a, grad_b, jnp.sum(loss[0])


def solution(mesh):
    fine = Mesh(mesh.devices.reshape(SIZES), AXES)
    spec = P(("yh", "z"), ("x", "yl", "c"))
    return jax.shard_map(
        body, mesh=fine, in_specs=(spec, spec), out_specs=(spec, spec, P()), check_vma=False
    )
```

```python
import jax
import jax.numpy as jnp
from jax import lax
from jax.sharding import Mesh, PartitionSpec as P

D = 8192
F32 = jnp.float32
BF16 = jnp.bfloat16
AXES = ("yh", "z", "x", "yl", "c")
SIZES = (2, 4, 4, 2, 2)
COUNT = dict(zip(AXES, SIZES, strict=True))


def shift(value, axis, step):
    size = COUNT[axis]
    return lax.ppermute(value, axis, [(i, (i + step) % size) for i in range(size)])


def gather_small(value, axes, size):
    return lax.all_to_all(jnp.broadcast_to(value, (size,) + value.shape), axes, 0, 0)


def swap(value, axis, mask):
    return lax.ppermute(value, axis, [(i, i ^ mask) for i in range(COUNT[axis])])


def batch_shift(value, half, step):
    pairs = [(4 * y + z, 4 * (y ^ half) + (z + step) % 4) for y in range(2) for z in range(4)]
    return lax.ppermute(value, ("yh", "z"), pairs)


def nt(lhs, rhs):
    return lax.dot_general(lhs, rhs, (((1,), (1,)), ((), ())), preferred_element_type=F32)


def send_gram(part):
    pieces = part.reshape(8, part.shape[0] // 8, part.shape[1])
    return lax.all_to_all(pieces, ("x", "yl"), 0, 0)


def sum_gram(got):
    return jnp.sum(got.astype(F32), axis=0)


def spread_gram(low):
    other = shift(low, "yl", 1)
    first = lax.axis_index("yl") == 0
    return jnp.stack([jnp.where(first, low, other), jnp.where(first, other, low)])


def gather_gram(both):
    n = both.shape[2]
    prev = shift(both, "x", 1)
    succ = shift(both, "x", 3)
    far0 = shift(prev[0], "x", 1)
    far1 = shift(succ[1], "x", 3)
    x = lax.axis_index("x")
    rows = jnp.zeros((4, 2, 64, n), BF16)
    for step, block in ((0, both), (3, prev), (1, succ), (2, jnp.stack([far0, far1]))):
        rows = lax.dynamic_update_slice_in_dim(rows, block[None], (x + step) % 4, 0)
    return rows.reshape(512, n), prev, far0


def place(x, own, prev, opposite, succ):
    rows = jnp.zeros((4,) + own.shape, own.dtype)
    for step, block in ((0, own), (3, prev), (2, opposite), (1, succ)):
        rows = lax.dynamic_update_slice_in_dim(rows, block[None], (x + step) % 4, 0)
    return rows


def merge(stats, axis, mask, held):
    apart = swap(stats, axis, mask)
    gap = (stats[0] - apart[0]) / held
    return jnp.stack([stats[0] + apart[0], stats[1] + apart[1] + gap * gap * (held / 2)])


def body(view_a, view_b):
    rows = view_a.shape[0]
    samples = 4096
    divisor = float(samples - 1)
    core0 = lax.axis_index("c") == 0

    got_a = shift(view_a, "c", 1)
    got_b = shift(view_b, "c", 1)
    mine = jnp.concatenate(
        [jnp.where(core0, view_a, view_b), jnp.where(core0, got_a, got_b)], axis=1
    )
    other = jnp.concatenate(
        [jnp.where(core0, view_b, view_a), jnp.where(core0, got_b, got_a)], axis=1
    )

    mine32 = mine.astype(F32)
    local_sum = jnp.sum(mine32, axis=0)
    local_dev = mine32 - local_sum / rows
    local_square = jnp.sum(local_dev * local_dev, axis=0)
    stats = jnp.stack([local_sum, local_square])
    everyone = [stats] + [shift(stats, "z", step) for step in (1, 3, 2)]
    total = sum(one[0] for one in everyone)
    gaps = [one[0] / 512.0 - total / 2048.0 for one in everyone]
    spread = sum(one[1] + 512.0 * gap * gap for one, gap in zip(everyone, gaps, strict=True))
    stats = jnp.stack([total, spread])
    ring, stats = lax.optimization_barrier((mine, stats))
    stats = merge(stats, "yh", 1, 2048.0)
    sent, stats = lax.optimization_barrier((mine, stats))
    mean = stats[0] / samples
    var = stats[1] / divisor
    std = jnp.sqrt(var + 0.0001)

    left = shift(ring, "z", 1)
    right = shift(ring, "z", 3)
    partner = shift(sent, "yh", 1)
    far0 = shift(left[:256], "z", 1)
    far1 = shift(right[256:], "z", 3)

    def centre(value, mean):
        return (value.astype(F32) - mean).astype(BF16)

    cent = mine32 - mean
    own = cent.astype(BF16)
    part = nt(own, own).astype(BF16).reshape(4, 128, 512)
    got_self = lax.all_to_all(part, "x", 0, 0)
    partner, right, mean0, got_self = lax.optimization_barrier((partner, right, mean, got_self))
    pair = centre(partner, mean0)
    after = centre(right, mean0)
    near = jnp.concatenate([own, after])
    far0, far1, mean1 = lax.optimization_barrier((far0, far1, mean0))
    far = jnp.concatenate([centre(far0, mean1), centre(far1, mean1)])
    rows = jnp.stack([pair.reshape(8, 64, 1024), own.reshape(8, 64, 1024)], axis=1)
    part_far = nt(rows.reshape(1024, 1024), far).astype(BF16)
    part = jnp.concatenate([nt(pair, near), nt(own, after)], axis=1).astype(BF16)
    got_near = send_gram(part)
    part_far, got_near, mean2, left = lax.optimization_barrier((part_far, got_near, mean1, left))
    got_far = send_gram(part_far)
    before = centre(left, mean2)
    got_near, got_own = got_near[:, :, :1024], got_near[:, :, 1024:]

    red_near = sum_gram(got_near)
    low_near = red_near.astype(BF16)
    turned_near = batch_shift(low_near[:, 512:], 1, 1)
    got_far, low_near = lax.optimization_barrier((got_far, low_near))
    x = lax.axis_index("x")
    first = lax.axis_index("yl") == 0
    opposite = shift(low_near, "x", 2)
    here = place(x, low_near, shift(low_near, "x", 1), opposite, shift(low_near, "x", 3))
    there = shift(here, "yl", 1)
    gram_near = jnp.stack([jnp.where(first, here, there), jnp.where(first, there, here)], axis=1)
    gram_near = gram_near.reshape(512, 1024)
    red_far = sum_gram(got_far)
    low_far = red_far.astype(BF16)
    low_pair = jnp.concatenate([low_far[:64], turned_near], axis=1)
    both_pair = spread_gram(low_pair)
    red_self, red_own = sum_gram(got_self), sum_gram(got_own)
    even = lax.axis_index("yl") == 0
    rest = jnp.where(even, red_self[64:], red_self[:64]).astype(BF16)
    red_self = jnp.where(even, red_self[:64], red_self[64:]) + shift(rest, "yl", 1).astype(F32)
    low_own = red_own.astype(BF16)
    turned_own = batch_shift(low_own, 0, 1)
    low_own = jnp.concatenate(
        [red_self.astype(BF16), low_own, low_far[64:], turned_own], axis=1
    )

    def lanes(value):
        return jnp.sum(value.reshape(-1, 128), axis=0)

    def rows_of(value):
        return lanes(jnp.sum(value, axis=0))

    frobenius = (
        rows_of(red_far * red_far)
        + rows_of(red_self * red_self)
        + rows_of(red_near[:, :512] * red_near[:, :512])
        + 2.0 * rows_of(red_near[:, 512:] * red_near[:, 512:] + red_own * red_own)
    )
    diff = view_a.astype(F32) - view_b.astype(F32)
    column_part = lanes(12.5 * jax.nn.relu(1.0 - std) - var * var)
    loss = (
        rows_of(diff * diff) * (25.0 / (samples * D))
        + column_part * (1.0 / (D * 8))
        + frobenius * (1.0 / (divisor * divisor * D))
    )
    high = lax.reduce_precision(loss, 8, 7)
    middle = lax.reduce_precision(loss - high, 8, 7)
    low = loss - high - middle
    line = lax.broadcasted_iota(jnp.int32, (64, 128), 0)
    loss = jnp.where(line == 0, high, jnp.where(line == 1, middle, jnp.where(line == 2, low, 0.0)))
    first = lax.axis_index("yl") == 0
    zeros = jnp.zeros((64, 128), BF16)
    loss = loss.astype(BF16)
    loss = jnp.stack([jnp.where(first, loss, zeros), jnp.where(first, zeros, loss)])
    both_pair = jnp.concatenate([both_pair, loss], axis=2)

    three = jnp.concatenate([near, far])

    def times(gram, start, stop):
        return jnp.dot(
            gram[:, :1536], three[:, start:stop], preferred_element_type=F32
        ) + lax.dot_general(
            gram[:, 1536:2048],
            before[:, start:stop],
            (((0,), (0,)), ((), ())),
            preferred_element_type=F32,
        )

    gram_pair, _, came = gather_gram(both_pair)
    cols = view_a.shape[1]
    inner_near = jnp.dot(gram_near, near, preferred_element_type=F32)
    inner_near, gram_pair = lax.optimization_barrier((inner_near, gram_pair))
    inner_pair = (
        inner_near
        + jnp.dot(gram_pair[:, :512], far, preferred_element_type=F32)
        + lax.dot_general(
            gram_pair[:, 512:1024], before, (((0,), (0,)), ((), ())), preferred_element_type=F32
        )
    ).astype(BF16)
    loss = jnp.sum(gram_pair.reshape(8, 64, 1152)[:, :3, 1024:].astype(F32), axis=(0, 1))
    loss = jnp.broadcast_to(loss, (8, 128))
    loss = loss + swap(loss, "yl", 1)
    inner_pair, loss = lax.optimization_barrier((inner_pair, loss))
    from_pair = shift(inner_pair, "yh", 1)
    both_own, _ = lax.optimization_barrier((spread_gram(low_own), came))
    gram_own, came, _ = gather_gram(both_own)
    loss, _ = lax.optimization_barrier((loss, came))
    for axis, mask in (("z", 1), ("z", 3)):
        loss = loss + swap(loss, axis, mask)
    inner_own, loss = lax.optimization_barrier((times(gram_own, 0, 2 * cols), loss))
    loss = loss + swap(loss, "yh", 1)
    from_pair, loss = lax.optimization_barrier((from_pair, loss))

    ratio = samples / divisor
    weight = 3.125 * ratio * jnp.where(std < 1.0, 1.0 / std, 0.0)

    inner = (inner_own + from_pair.astype(F32)) / divisor
    term = ratio * (inner - cent * var) - weight * cent
    grad = (term + 12.5 * (mine32 - other.astype(F32))).astype(BF16)
    back = shift(grad[:, cols:], "c", 1)
    keep = grad[:, :cols]
    grad_a = jnp.where(core0, keep, back)
    grad_b = jnp.where(core0, back, keep)

    loss = loss + swap(loss, "c", 1)
    return grad_a, grad_b, jnp.sum(loss[0])


def solution(mesh):
    fine = Mesh(mesh.devices.reshape(SIZES), AXES)
    spec = P(("yh", "z"), ("x", "yl", "c"))
    return jax.shard_map(
        body, mesh=fine, in_specs=(spec, spec), out_specs=(spec, spec, P()), check_vma=False
    )
```

```python
import jax
import jax.numpy as jnp
from jax import lax
from jax.sharding import Mesh, PartitionSpec as P

D = 8192
F32 = jnp.float32
BF16 = jnp.bfloat16
AXES = ("yh", "z", "x", "yl", "c")
SIZES = (2, 4, 4, 2, 2)
COUNT = dict(zip(AXES, SIZES, strict=True))


def shift(value, axis, step):
    size = COUNT[axis]
    return lax.ppermute(value, axis, [(i, (i + step) % size) for i in range(size)])


def gather_small(value, axes, size):
    return lax.all_to_all(jnp.broadcast_to(value, (size,) + value.shape), axes, 0, 0)


def swap(value, axis, mask):
    return lax.ppermute(value, axis, [(i, i ^ mask) for i in range(COUNT[axis])])


def batch_shift(value, half, step):
    pairs = [(4 * y + z, 4 * (y ^ half) + (z + step) % 4) for y in range(2) for z in range(4)]
    return lax.ppermute(value, ("yh", "z"), pairs)


def nt(lhs, rhs):
    return lax.dot_general(lhs, rhs, (((1,), (1,)), ((), ())), preferred_element_type=F32)


def send_gram(part):
    pieces = part.reshape(8, part.shape[0] // 8, part.shape[1])
    return lax.all_to_all(pieces, ("x", "yl"), 0, 0)


def sum_gram(got):
    return jnp.sum(got.astype(F32), axis=0)


def spread_gram(low):
    other = shift(low, "yl", 1)
    first = lax.axis_index("yl") == 0
    return jnp.stack([jnp.where(first, low, other), jnp.where(first, other, low)])


def gather_gram(both):
    n = both.shape[2]
    prev = shift(both, "x", 1)
    succ = shift(both, "x", 3)
    far0 = shift(prev[0], "x", 1)
    far1 = shift(succ[1], "x", 3)
    x = lax.axis_index("x")
    rows = jnp.zeros((4, 2, 64, n), BF16)
    for step, block in ((0, both), (3, prev), (1, succ), (2, jnp.stack([far0, far1]))):
        rows = lax.dynamic_update_slice_in_dim(rows, block[None], (x + step) % 4, 0)
    return rows.reshape(512, n), prev, far1


def place(x, own, prev, opposite, succ):
    rows = jnp.zeros((4,) + own.shape, own.dtype)
    for step, block in ((0, own), (3, prev), (2, opposite), (1, succ)):
        rows = lax.dynamic_update_slice_in_dim(rows, block[None], (x + step) % 4, 0)
    return rows


def merge(stats, axis, mask, held):
    apart = swap(stats, axis, mask)
    gap = (stats[0] - apart[0]) / held
    return jnp.stack([stats[0] + apart[0], stats[1] + apart[1] + gap * gap * (held / 2)])


def body(view_a, view_b):
    rows = view_a.shape[0]
    samples = 4096
    divisor = float(samples - 1)
    core0 = lax.axis_index("c") == 0

    got_a = shift(view_a, "c", 1)
    got_b = shift(view_b, "c", 1)
    mine = jnp.concatenate(
        [jnp.where(core0, view_a, view_b), jnp.where(core0, got_a, got_b)], axis=1
    )
    other = jnp.concatenate(
        [jnp.where(core0, view_b, view_a), jnp.where(core0, got_b, got_a)], axis=1
    )

    mine32 = mine.astype(F32)
    local_sum = jnp.sum(mine32, axis=0)
    local_dev = mine32 - local_sum / rows
    local_square = jnp.sum(local_dev * local_dev, axis=0)
    stats = jnp.stack([local_sum, local_square])
    everyone = [stats] + [shift(stats, "z", step) for step in (1, 3, 2)]
    total = sum(one[0] for one in everyone)
    gaps = [one[0] / 512.0 - total / 2048.0 for one in everyone]
    spread = sum(one[1] + 512.0 * gap * gap for one, gap in zip(everyone, gaps, strict=True))
    stats = jnp.stack([total, spread])
    ring, stats = lax.optimization_barrier((mine, stats))
    stats = merge(stats, "yh", 1, 2048.0)
    sent, stats = lax.optimization_barrier((mine, stats))
    mean = stats[0] / samples
    var = stats[1] / divisor
    std = jnp.sqrt(var + 0.0001)

    left = shift(ring, "z", 1)
    right = shift(ring, "z", 3)
    partner = shift(sent, "yh", 1)
    far0 = shift(left[:256], "z", 1)
    far1 = shift(right[256:], "z", 3)

    def centre(value, mean):
        return (value.astype(F32) - mean).astype(BF16)

    cent = mine32 - mean
    own = cent.astype(BF16)
    part = nt(own, own).astype(BF16).reshape(4, 128, 512)
    got_self = lax.all_to_all(part, "x", 0, 0)
    partner, right, mean0, got_self = lax.optimization_barrier((partner, right, mean, got_self))
    pair = centre(partner, mean0)
    after = centre(right, mean0)
    near = jnp.concatenate([own, after])
    far0, far1, mean1 = lax.optimization_barrier((far0, far1, mean0))
    far = jnp.concatenate([centre(far0, mean1), centre(far1, mean1)])
    rows = jnp.stack([pair.reshape(8, 64, 1024), own.reshape(8, 64, 1024)], axis=1)
    part_far = nt(rows.reshape(1024, 1024), far).astype(BF16)
    part = jnp.concatenate([nt(pair, near), nt(own, after)], axis=1).astype(BF16)
    got_near = send_gram(part)
    part_far, got_near, mean2, left = lax.optimization_barrier((part_far, got_near, mean1, left))
    got_far = send_gram(part_far)
    before = centre(left, mean2)
    got_near, got_own = got_near[:, :, :1024], got_near[:, :, 1024:]

    red_near = sum_gram(got_near)
    low_near = red_near.astype(BF16)
    turned_near = batch_shift(low_near[:, 512:], 1, 1)
    got_far, low_near = lax.optimization_barrier((got_far, low_near))
    x = lax.axis_index("x")
    first = lax.axis_index("yl") == 0
    opposite, succ = shift(low_near, "x", 2), shift(low_near, "x", 3)
    here = place(x, low_near, shift(low_near, "x", 1), opposite, succ)
    there = shift(here, "yl", 1)
    gram_near = jnp.stack([jnp.where(first, here, there), jnp.where(first, there, here)], axis=1)
    gram_near = gram_near.reshape(512, 1024)
    red_far = sum_gram(got_far)
    low_far = red_far.astype(BF16)
    low_pair = jnp.concatenate([low_far[:64], turned_near], axis=1)
    both_pair = spread_gram(low_pair)
    red_self, red_own = sum_gram(got_self), sum_gram(got_own)
    even = lax.axis_index("yl") == 0
    rest = jnp.where(even, red_self[64:], red_self[:64]).astype(BF16)
    red_self = jnp.where(even, red_self[:64], red_self[64:]) + shift(rest, "yl", 1).astype(F32)
    low_own = red_own.astype(BF16)
    turned_own = batch_shift(low_own, 0, 1)
    low_own = jnp.concatenate(
        [red_self.astype(BF16), low_own, low_far[64:], turned_own], axis=1
    )

    def lanes(value):
        return jnp.sum(value.reshape(-1, 128), axis=0)

    def rows_of(value):
        return lanes(jnp.sum(value, axis=0))

    frobenius = (
        rows_of(red_far * red_far)
        + rows_of(red_self * red_self)
        + rows_of(red_near[:, :512] * red_near[:, :512])
        + 2.0 * rows_of(red_near[:, 512:] * red_near[:, 512:] + red_own * red_own)
    )
    diff = view_a.astype(F32) - view_b.astype(F32)
    column_part = lanes(12.5 * jax.nn.relu(1.0 - std) - var * var)
    loss = (
        rows_of(diff * diff) * (25.0 / (samples * D))
        + column_part * (1.0 / (D * 8))
        + frobenius * (1.0 / (divisor * divisor * D))
    )
    high = lax.reduce_precision(loss, 8, 7)
    middle = lax.reduce_precision(loss - high, 8, 7)
    low = loss - high - middle
    line = lax.broadcasted_iota(jnp.int32, (64, 128), 0)
    loss = jnp.where(line == 0, high, jnp.where(line == 1, middle, jnp.where(line == 2, low, 0.0)))
    first = lax.axis_index("yl") == 0
    zeros = jnp.zeros((64, 128), BF16)
    loss = loss.astype(BF16)
    loss = jnp.stack([jnp.where(first, loss, zeros), jnp.where(first, zeros, loss)])
    both_pair = jnp.concatenate([both_pair, loss], axis=2)

    three = jnp.concatenate([near, far])

    def times(gram, start, stop):
        return jnp.dot(
            gram[:, :1536], three[:, start:stop], preferred_element_type=F32
        ) + lax.dot_general(
            gram[:, 1536:2048],
            before[:, start:stop],
            (((0,), (0,)), ((), ())),
            preferred_element_type=F32,
        )

    gram_pair, _, came = gather_gram(both_pair)
    cols = view_a.shape[1]
    inner_near = jnp.dot(gram_near, near, preferred_element_type=F32)
    inner_near, gram_pair = lax.optimization_barrier((inner_near, gram_pair))
    inner_pair = (
        inner_near
        + jnp.dot(gram_pair[:, :512], far, preferred_element_type=F32)
        + lax.dot_general(
            gram_pair[:, 512:1024], before, (((0,), (0,)), ((), ())), preferred_element_type=F32
        )
    ).astype(BF16)
    loss = jnp.sum(gram_pair.reshape(8, 64, 1152)[:, :3, 1024:].astype(F32), axis=(0, 1))
    loss = jnp.broadcast_to(loss, (8, 128))
    loss = loss + swap(loss, "yl", 1)
    inner_pair, loss = lax.optimization_barrier((inner_pair, loss))
    from_pair = shift(inner_pair, "yh", 1)
    both_own, _ = lax.optimization_barrier((spread_gram(low_own), came))
    gram_own, came, _ = gather_gram(both_own)
    loss, _ = lax.optimization_barrier((loss, came))
    for axis, mask in (("z", 1), ("z", 3)):
        loss = loss + swap(loss, axis, mask)
    inner_own, loss = lax.optimization_barrier((times(gram_own, 0, 2 * cols), loss))
    loss = loss + swap(loss, "yh", 1)
    from_pair, loss = lax.optimization_barrier((from_pair, loss))

    ratio = samples / divisor
    weight = 3.125 * ratio * jnp.where(std < 1.0, 1.0 / std, 0.0)

    inner = (inner_own + from_pair.astype(F32)) / divisor
    term = ratio * (inner - cent * var) - weight * cent
    grad = (term + 12.5 * (mine32 - other.astype(F32))).astype(BF16)
    back = shift(grad[:, cols:], "c", 1)
    keep = grad[:, :cols]
    grad_a = jnp.where(core0, keep, back)
    grad_b = jnp.where(core0, back, keep)

    loss = loss + swap(loss, "c", 1)
    return grad_a, grad_b, jnp.sum(loss[0])


def solution(mesh):
    fine = Mesh(mesh.devices.reshape(SIZES), AXES)
    spec = P(("yh", "z"), ("x", "yl", "c"))
    return jax.shard_map(
        body, mesh=fine, in_specs=(spec, spec), out_specs=(spec, spec, P()), check_vma=False
    )
```
